32 devices in a mesh: dp: 4 (over y, x), expert: 8 (over z, core).
Axes of the slice: x: 2, y: 2, z: 4, core: 2. Of those that a mesh axis runs over, the one named last changes fastest.
Arguments:
- tokens: bfloat16 [2048, 4096], P(('dp', 'expert')), may hold values from -6 to 6
- routes: int32 [2048, 8], P(('dp', 'expert')), may hold values from 0 to 15, all different within a row; in each aligned block of 64 rows (0 to 63, 64 to 127, ...) at most 42 rows name the same one
- gate_fixed: int32 [2048, 8], P(('dp', 'expert')), may hold values from 1 to 65535
- w_gate: bfloat16 [32, 4096, 768], P(('dp', 'expert')), may hold values from -0.09375 to 0.09375
- w_up: bfloat16 [32, 4096, 768], P(('dp', 'expert')), may hold values from -0.09375 to 0.09375
- w_down: bfloat16 [32, 768, 4096], P(('dp', 'expert')), may hold values from -0.15625 to 0.15625
Outputs:
- mixed: bfloat16 [2048, 4096], P(('dp', 'expert'))
The draws below stay inside these ranges and needn't reach their ends.
Inputs may be any that keep to these rules, and one draw needn't show every extreme that they name: `routes`: each row names 8 different experts. In each aligned block of 64 rows (the rows of one device) no expert is named by more than 42 rows, and in some block one expert is named by exactly 42 rows.
All inputs are finite; a program needn't handle non-finite values.
Results may differ from the reference program's by a relative error of at most 0.0058.
Values may be sent and summed in bfloat16 or wider, within the bound.
No kernel may reach another device: no remote copies, remote signals or barrier semaphores. Data moves between devices by JAX's collectives and lax.ppermute only.
A program may use at most 192 MiB of HBM per device.

```python
import math
import jax
import jax.numpy as jnp
import numpy as np
from jax import lax

D = 4096
FF = 1536
TOP = 8
TOK_DEV = 64
HALF = 768
EXPERTS = 16
CAP = 42
TOKENS = 2048
N_DP = 4
N_EXPERT = 8


def with_ends(array, key, smallest, high):
    index_at = [jax.random.randint(jax.random.fold_in(key, axis), (), 0, length) for axis, length in enumerate(array.shape)]
    widest = array.shape.index(max(array.shape))
    next_to = index_at[:widest] + [(index_at[widest] + 1) % array.shape[widest]] + index_at[widest + 1:]
    return array.at[tuple(index_at)].set(smallest).at[tuple(next_to)].set(high)


def block_levels(own_key, extent, shards, smallest, high):
    factor_of = 1.0
    for axis_at, blocks in shards:
        draws = jax.random.uniform(jax.random.fold_in(jax.random.fold_in(own_key, 6), axis_at), (blocks,), jnp.float32, smallest / len(shards), high / len(shards))
        factor_of = factor_of * jnp.repeat(jnp.exp(draws), extent[axis_at] // blocks).reshape((-1,) + (1,) * (len(extent) - 1 - axis_at))
    return factor_of


def assign_block(rng, own, number, rows, count, top, reach, lean):
    ranking = jax.random.permutation(rng, count)
    packed, usual = shares(count, rows * top, reach, lean, True), shares(count, rows * top, reach, lean, False)
    places = jnp.arange(count)

    def named(sizes, turn):
        used = int((sizes > 0).sum())
        fixed = max(1, used // 4)
        moved = fixed + (places - fixed + turn * (used - fixed)) % max(1, count - fixed)
        return jnp.zeros((count,), jnp.int32).at[ranking[jnp.where(places < fixed, places, moved)]].set(jnp.asarray(sizes, jnp.int32))

    sizes = jnp.where(number % 4 == 0, named(packed, number // 4), named(usual, number - number // 4 - 1))
    mixed = jax.random.permutation(jax.random.fold_in(own, 3), count)
    donor, sink = mixed[0:count // 2 * 2:2], mixed[1:count // 2 * 2:2]
    slack = jnp.minimum(sizes[donor] - 1, reach - sizes[sink]) // 2
    slack = jnp.where((donor == ranking[0]) | (sink == ranking[0]) | (sizes[sink] == 0), 0, jnp.maximum(slack, 0))
    moved = jax.random.randint(jax.random.fold_in(own, 4), (count // 2,), 0, 1 << 20) % (slack + 1)
    sizes = sizes.at[donor].add(-moved).at[sink].add(moved)
    items = jnp.searchsorted(jnp.cumsum(sizes), jnp.arange(rows * top), side="right").astype(jnp.int32)
    table = items.reshape(top, rows).T
    table = table[jax.random.permutation(jax.random.fold_in(own, 1), rows)]
    turn = jax.random.randint(jax.random.fold_in(own, 2), (rows, 1), 0, top)
    return jnp.take_along_axis(table, (jnp.arange(top)[None, :] + turn) % top, axis=1)


def shares(amount, total, reach, skew, full):
    weights = [(1 << 20) // math.isqrt(standing ** skew) + 1 for standing in range(1, amount + 1)]
    largest = reach if full else min(reach, max(-(-total // amount), total * weights[0] // sum(weights)))
    least = 1 if total - largest >= amount - 1 else 0
    holding, spare = [largest] + [least] * (amount - 1), total - largest - least * (amount - 1)
    while spare > 0:
        candidates = [i for i in range(1, amount) if holding[i] < largest] or [i for i in range(1, amount) if holding[i] < reach]
        mass, budget = sum([weights[i] for i in candidates]), spare
        for i in candidates:
            extra = min(reach - holding[i], max(1, budget * weights[i] // mass), spare)
            holding[i] = holding[i] + extra
            spare = spare - extra
    return np.array(holding)


def normal_values(rng, extent, deviation, bound, shards=(), held_as=jnp.bfloat16):
    level = block_levels(rng, extent, shards, -0.22, 0.18) if shards else 1.0
    values = jax.random.normal(rng, extent, jnp.float32) * deviation * level
    return jnp.minimum(jnp.maximum(values, -bound), bound).astype(held_as)


def setup_inputs(seed: int = 0) -> dict:
    keys = jax.random.split(jax.random.key(seed), 7)
    tokens = normal_values(keys[0], (TOKENS, D), 1.0, 6.0, ((0, 32),))
    routes_keys = jax.random.split(jax.random.fold_in(keys[1], 1), TOKENS // TOK_DEV)
    routes_turns = jax.random.permutation(jax.random.fold_in(keys[1], 3), TOKENS // TOK_DEV)
    routes = jax.vmap(lambda own, number: assign_block(jax.random.fold_in(keys[1], 2), own, number, TOK_DEV, EXPERTS, TOP, CAP, 2))(routes_keys, routes_turns).reshape((TOKENS, TOP))
    gate_fixed = with_ends(jax.random.randint(keys[2], (TOKENS, TOP), 1, 65536), jax.random.fold_in(keys[2], 1), 1, 65535).astype(jnp.int32)
    w_gate = normal_values(keys[3], (2 * EXPERTS, D, HALF), D ** -0.5, 0.09375, ((0, 32),))
    w_up = normal_values(keys[4], (2 * EXPERTS, D, HALF), D ** -0.5, 0.09375, ((0, 32),))
    w_down = normal_values(keys[5], (2 * EXPERTS, HALF, D), FF ** -0.5, 0.15625, ((0, 32),))
    return {"tokens": tokens, "routes": routes, "gate_fixed": gate_fixed, "w_gate": w_gate, "w_up": w_up, "w_down": w_down}


def reference(tokens, routes, gate_fixed, w_gate, w_up, w_down):
    sources = N_DP * N_EXPERT
    quant = gate_fixed.astype(jnp.float32)
    weights = quant / jnp.sum(quant, axis=1, keepdims=True)
    blocks = routes.reshape(sources, TOK_DEV * TOP)
    onehot = (blocks[:, :, None] == jnp.arange(EXPERTS, dtype=jnp.int32)[None, None, :]).astype(jnp.int32)
    before = jnp.cumsum(onehot, axis=1) - onehot
    slot = jnp.sum(before * onehot, axis=2)
    source_ids = jnp.arange(sources, dtype=jnp.int32)[:, None]
    place = (blocks * sources + source_ids) * CAP + slot
    token_ids = source_ids * TOK_DEV + (jnp.arange(TOK_DEV * TOP, dtype=jnp.int32) // TOP)[None, :]
    table = jnp.full((EXPERTS * sources * CAP,), TOKENS, jnp.int32).at[place.reshape(-1)].set(token_ids.reshape(-1))
    factor = jnp.zeros((EXPERTS * sources * CAP,), jnp.float32).at[place.reshape(-1)].set(weights.reshape(-1))
    padded = jnp.concatenate([tokens, jnp.zeros((1, D), tokens.dtype)], axis=0)
    gate_pairs = w_gate.reshape(EXPERTS, 2, D, HALF)
    up_pairs = w_up.reshape(EXPERTS, 2, D, HALF)
    down_pairs = w_down.reshape(EXPERTS, 2, HALF, D)

    def one_expert(total, items):
        index, scale, gate_pair, up_pair, down_pair = items
        rows = padded[index]
        gate_full = jnp.concatenate([gate_pair[0], gate_pair[1]], axis=1)
        up_full = jnp.concatenate([up_pair[0], up_pair[1]], axis=1)
        down_full = jnp.concatenate([down_pair[0], down_pair[1]], axis=0)
        gate = jnp.dot(rows, gate_full, preferred_element_type=jnp.float32)
        upper = jnp.dot(rows, up_full, preferred_element_type=jnp.float32)
        hidden = (jax.nn.silu(gate) * upper).astype(jnp.bfloat16)
        result = jnp.dot(hidden, down_full, preferred_element_type=jnp.float32).astype(jnp.bfloat16)
        total = total.at[index].add(scale[:, None] * result.astype(jnp.float32))
        return total, None

    start = jnp.zeros((TOKENS + 1, D), jnp.float32)
    items = (table.reshape(EXPERTS, sources * CAP), factor.reshape(EXPERTS, sources * CAP), gate_pairs, up_pairs, down_pairs)
    total, _ = lax.scan(one_expert, start, items)
    return total[:TOKENS].astype(jnp.bfloat16)
```

```python
import functools

import jax
import jax.numpy as jnp
from jax import lax
from jax.experimental import pallas as pl
from jax.experimental.pallas import tpu as pltpu
from jax.sharding import PartitionSpec as P

TOP = 8
FOLD = 8
TILE = 256
F32 = jnp.float32
BF16 = jnp.bfloat16


def iota(shape, dim):
    return lax.broadcasted_iota(jnp.int32, shape, dim)


def padded(cap):
    return -(-cap // 16) * 16


def slot_codes(weights):
    rows = weights.shape[0]
    named = weights > 0.0
    tri = (iota((rows, rows), 0) > iota((rows, rows), 1)).astype(BF16)
    slots = jnp.dot(tri, named.astype(BF16), preferred_element_type=F32)
    return jnp.where(named, slots, -1.0)


def column(values, which):
    return jnp.sum(jnp.where(iota(values.shape, 1) == which, values, 0.0), axis=1, keepdims=True)


def pack_kernel(ids_ref, x_ref, w_ref, *out_refs):
    rows, width = x_ref.shape
    part = width // FOLD
    stacked = jnp.concatenate([x_ref[:, g * part : (g + 1) * part] for g in range(FOLD)], axis=0)
    codes = slot_codes(w_ref[...])
    for m, out_ref in enumerate(out_refs):
        col = column(codes, ids_ref[m])
        spread = (rows, FOLD * rows)
        row = jnp.sum(
            jnp.where(iota(spread, 0) == iota(spread, 1) % rows, col, 0.0), axis=0, keepdims=True
        ).astype(jnp.int32)
        shape = (out_ref.shape[0], FOLD * rows)
        r, c = iota(shape, 0), iota(shape, 1)
        pick = ((r % FOLD == c // rows) & (row == r // FOLD)).astype(BF16)
        out_ref[...] = jnp.dot(pick, stacked, preferred_element_type=F32).astype(BF16)


def pack(x, weights, ids, cap):
    rows, width = x.shape
    n = ids.shape[0]
    shape = jax.ShapeDtypeStruct((cap * FOLD, width // FOLD), x.dtype)
    vmem = pl.BlockSpec(memory_space=pltpu.VMEM)
    return pl.pallas_call(
        pack_kernel,
        out_shape=(shape,) * n,
        in_specs=[pl.BlockSpec(memory_space=pltpu.SMEM), vmem, vmem],
        out_specs=(vmem,) * n,
        compiler_params=pltpu.CompilerParams(vmem_limit_bytes=48 << 20),
        name="pack",
    )(ids, x, weights)


def expert_kernel(n, cap, *refs):
    blocks, refs = refs[:n], refs[n:]
    (g_a, u_a, d_a, g_b, u_b, d_b), refs = refs[:6], refs[6:]
    outs, refs = refs[:n], refs[n:]
    x_ref, acc_ref, g_buf, u_buf, d_buf, sems = refs
    half = g_a.shape[2]
    part = x_ref.shape[1] // FOLD
    high = padded(cap)
    steps = [(s, j) for s in ((g_a, u_a, d_a), (g_b, u_b, d_b)) for j in range(half // TILE)]
    depth = g_buf.shape[0]

    def copies(i):
        (g, u, d), j = steps[i]
        slot = i % depth
        hidden = pl.ds(j * TILE, TILE)
        return [
            pltpu.make_async_copy(g.at[0, :, hidden], g_buf.at[slot], sems.at[slot, 0]),
            pltpu.make_async_copy(u.at[0, :, hidden], u_buf.at[slot], sems.at[slot, 1]),
            pltpu.make_async_copy(d.at[0, hidden, :], d_buf.at[slot], sems.at[slot, 2]),
        ]

    for i in range(depth - 1):
        for copy in copies(i):
            copy.start()
    shape = (FOLD * high, FOLD * cap)
    r, c = iota(shape, 0), iota(shape, 1)
    spread = ((c % FOLD == r // high) & (c // FOLD == r % high)).astype(BF16)
    for m in range(n):
        rows = jnp.dot(spread, blocks[m][...], preferred_element_type=F32).astype(BF16)
        for g in range(FOLD):
            x_ref[m * high : (m + 1) * high, g * part : (g + 1) * part] = rows[
                g * high : (g + 1) * high
            ]
    for i in range(len(steps)):
        if i + depth - 1 < len(steps):
            for copy in copies(i + depth - 1):
                copy.start()
        for copy in copies(i):
            copy.wait()
        slot = i % depth
        x = x_ref[...]
        gate = jnp.dot(x, g_buf[slot], preferred_element_type=F32)
        upper = jnp.dot(x, u_buf[slot], preferred_element_type=F32)
        hidden = (gate / (1.0 + jnp.exp(-gate)) * upper).astype(BF16)
        added = jnp.dot(hidden, d_buf[slot], preferred_element_type=F32)
        if i == 0:
            acc_ref[...] = added
        else:
            acc_ref[...] += added
    shape = (FOLD * cap, FOLD * high)
    r, c = iota(shape, 0), iota(shape, 1)
    gather = ((r % FOLD == c // high) & (r // FOLD == c % high)).astype(BF16)
    for m in range(n):
        stacked = jnp.concatenate(
            [
                acc_ref[m * high : (m + 1) * high, g * part : (g + 1) * part].astype(BF16)
                for g in range(FOLD)
            ],
            axis=0,
        )
        outs[m][...] = jnp.dot(gather, stacked, preferred_element_type=F32).astype(BF16)


def expert(blocks, mine, other, cap):
    n = len(blocks)
    width = mine[0].shape[1]
    rows = n * padded(cap)
    depth = 3
    vmem = pl.BlockSpec(memory_space=pltpu.VMEM)
    hbm = pl.BlockSpec(memory_space=pl.ANY)
    return pl.pallas_call(
        functools.partial(expert_kernel, n, cap),
        out_shape=tuple(jax.ShapeDtypeStruct(b.shape, b.dtype) for b in blocks),
        in_specs=[vmem] * n + [hbm] * 6,
        out_specs=(vmem,) * n,
        scratch_shapes=[
            pltpu.VMEM((rows, width), BF16),
            pltpu.VMEM((rows, width), F32),
            pltpu.VMEM((depth, width, TILE), BF16),
            pltpu.VMEM((depth, width, TILE), BF16),
            pltpu.VMEM((depth, TILE, width), BF16),
            pltpu.SemaphoreType.DMA((depth, 3)),
        ],
        compiler_params=pltpu.CompilerParams(vmem_limit_bytes=56 << 20),
        name="expert",
    )(*blocks, *mine, *other)


def combine_kernel(n, ids_ref, w_ref, *refs):
    blocks, others, out_ref = refs[:n], refs[n:-1], refs[-1]
    rows, width = out_ref.shape
    part = width // FOLD
    weights = w_ref[...]
    codes = slot_codes(weights)
    total = None
    for m in range(n):
        code = column(codes, ids_ref[m]).astype(jnp.int32)
        weight = column(weights, ids_ref[m])
        code = jnp.concatenate([code] * FOLD, axis=0)
        weight = jnp.concatenate([weight] * FOLD, axis=0)
        shape = (FOLD * rows, blocks[m].shape[0])
        c, r = iota(shape, 0), iota(shape, 1)
        pick = ((r % FOLD == c // rows) & (code == r // FOLD)).astype(BF16)
        term = weight * jnp.dot(pick, blocks[m][...], preferred_element_type=F32)
        total = term if total is None else total + term
    for g in range(FOLD):
        piece = total[g * rows : (g + 1) * rows]
        for other in others:
            piece += other[:, g * part : (g + 1) * part].astype(F32)
        out_ref[:, g * part : (g + 1) * part] = piece.astype(BF16)


def combine(blocks, weights, ids, others=()):
    n = len(blocks)
    cells, part = blocks[0].shape
    vmem = pl.BlockSpec(memory_space=pltpu.VMEM)
    return pl.pallas_call(
        functools.partial(combine_kernel, n),
        out_shape=jax.ShapeDtypeStruct((weights.shape[0], part * FOLD), BF16),
        in_specs=[pl.BlockSpec(memory_space=pltpu.SMEM)] + [vmem] * (1 + n + len(others)),
        out_specs=vmem,
        compiler_params=pltpu.CompilerParams(vmem_limit_bytes=48 << 20),
        name="combine",
    )(ids, weights, *blocks, *others)


def on_device(tokens, routes, gate_fixed, w_gate, w_up, w_down):
    n_data = lax.axis_size("dp")
    n_owner = lax.axis_size("expert")
    line = n_owner // 2
    expert_count = n_data * line
    tok_rows = tokens.shape[0]
    cap = 2 * (5 * tok_rows * TOP // (8 * expert_count) + 1)
    dp = lax.axis_index("dp")
    z = lax.axis_index("expert") // 2
    ids = jnp.stack([(dp ^ m) * line + z for m in range(n_data)]).astype(jnp.int32)

    def along(block, step):
        pairs = [(i, (i + 2 * step) % n_owner) for i in range(n_owner)]
        return lax.ppermute(block, "expert", pairs)

    def across(block, m):
        return lax.ppermute(block, "dp", [(i, i ^ m) for i in range(n_data)])

    def swap(block):
        return lax.ppermute(block, "expert", [(i, i ^ 1) for i in range(n_owner)])

    quant = gate_fixed.astype(F32)
    chosen = quant / jnp.sum(quant, axis=1, keepdims=True)
    hit = routes[:, :, None] == jnp.arange(expert_count, dtype=jnp.int32)[None, None, :]
    weights = jnp.sum(jnp.where(hit, chosen[:, :, None], 0.0), axis=1)

    mine = (w_gate, w_up, w_down)
    other = tuple(swap(w) for w in mine)

    order = [0] + [k for k in range(1, line)]
    xs, ws, sent = {0: tokens}, {0: weights}, {}
    for k in range(1, line):
        ws[k] = along(weights, k)
        xs[k] = along(tokens, k)
    for k in order:
        packed = pack(xs[k], ws[k], ids, cap)
        sent[k] = [packed[0]] + [across(packed[m], m) for m in range(1, n_data)]
    result = {}
    for k in order:
        outs = expert(sent[k], mine, other, cap)
        result[k] = [outs[0]] + [across(outs[m], m) for m in range(1, n_data)]
    back = []
    for k in order[1:]:
        back.append(along(combine(result[k], ws[k], ids), -k))
    return combine(result[0], ws[0], ids, back)


def solution(mesh):
    placed = (
        P(("dp", "expert"), None),
        P(("dp", "expert"), None),
        P(("dp", "expert"), None),
        P(("dp", "expert"), None, None),
        P(("dp", "expert"), None, None),
        P(("dp", "expert"), None, None),
    )
    return jax.shard_map(
        on_device, mesh=mesh, in_specs=placed, out_specs=P(("dp", "expert"), None), check_vma=False
    )
```

```python
import functools

import jax
import jax.numpy as jnp
from jax import lax
from jax.experimental import pallas as pl
from jax.experimental.pallas import tpu as pltpu
from jax.sharding import PartitionSpec as P

TOP = 8
FOLD = 8
SUB = 16
TILE = 256
F32 = jnp.float32
BF16 = jnp.bfloat16
VMEM = pl.BlockSpec(memory_space=pltpu.VMEM)
SMEM = pl.BlockSpec(memory_space=pltpu.SMEM)
ANY = pl.BlockSpec(memory_space=pl.ANY)


def iota(shape, dim):
    return lax.broadcasted_iota(jnp.int32, shape, dim)


def heights(cap):
    main = cap // SUB * SUB
    tail = cap - main
    return main, tail, main + (SUB if tail else 0)


def unfold(block, cap, rows_ref, base):
    main, tail, high = heights(cap)
    part = block.shape[1]
    if tail:
        shape = (FOLD * SUB, FOLD * tail)
        r, c = iota(shape, 0), iota(shape, 1)
        spread = ((r % SUB < tail) & (c == r // SUB * tail + r % SUB)).astype(BF16)
        last = jnp.dot(spread, block[FOLD * main :, :], preferred_element_type=F32).astype(BF16)
    for g in range(FOLD):
        cols = slice(g * part, (g + 1) * part)
        if main:
            rows_ref[base : base + main, cols] = block[g * main : (g + 1) * main, :]
        if tail:
            rows_ref[base + main : base + high, cols] = last[g * SUB : (g + 1) * SUB]


def fold(rows_ref, base, cap, block):
    main, tail, high = heights(cap)
    part = block.shape[1]
    columns = [slice(g * part, (g + 1) * part) for g in range(FOLD)]
    if main:
        for g, cols in enumerate(columns):
            block[g * main : (g + 1) * main, :] = rows_ref[base : base + main, cols]
    if tail:
        last = jnp.concatenate([rows_ref[base + main : base + high, cols] for cols in columns], axis=0)
        shape = (FOLD * tail, FOLD * SUB)
        r, c = iota(shape, 0), iota(shape, 1)
        gather = ((c % SUB < tail) & (r == c // SUB * tail + c % SUB)).astype(BF16)
        block[FOLD * main :, :] = jnp.dot(gather, last, preferred_element_type=F32).astype(BF16)


def slot_codes(weights):
    rows = weights.shape[0]
    named = weights > 0.0
    tri = (iota((rows, rows), 0) > iota((rows, rows), 1)).astype(BF16)
    slots = jnp.dot(tri, named.astype(BF16), preferred_element_type=F32)
    return jnp.where(named, slots, -1.0)


def column(values, which):
    return jnp.sum(jnp.where(iota(values.shape, 1) == which, values, 0.0), axis=1, keepdims=True)


def pack_body(cap, ids_ref, x_ref, weights, outs, rows_ref):
    tokens = x_ref.shape[0]
    high = heights(cap)[2]
    codes = slot_codes(weights)
    square = (tokens, tokens)
    picks = []
    for m in range(len(outs)):
        col = column(codes, ids_ref[m])
        row = jnp.sum(
            jnp.where(iota(square, 0) == iota(square, 1), col, 0.0), axis=0, keepdims=True
        ).astype(jnp.int32)
        picks.append((iota((high, tokens), 0) == row).astype(BF16))
    pick = jnp.concatenate(picks, axis=0)
    rows_ref[...] = jnp.dot(pick, x_ref[...], preferred_element_type=F32).astype(BF16)
    for m, out in enumerate(outs):
        fold(rows_ref, m * high, cap, out)


def tie(value, *others):
    return lax.optimization_barrier((value, *others))[0]


def tail_width(expert_count):
    return -(-3 * expert_count // 128) * 128


def first_kernel(n, cap, ids_ref, x_ref, routes_ref, gate_ref, *refs):
    w_ref, wide_ref, outs, rows_ref = refs[0], refs[1], refs[2 : 2 + n], refs[2 + n]
    quant = gate_ref[...].astype(F32)
    chosen = quant / jnp.sum(quant, axis=1, keepdims=True)
    routes = routes_ref[...]
    experts = iota(w_ref.shape, 1)
    weights = jnp.zeros(w_ref.shape, F32)
    for k in range(TOP):
        weights += jnp.where(experts == routes[:, k : k + 1], chosen[:, k : k + 1], 0.0)
    w_ref[...] = weights
    width, count = x_ref.shape[1], w_ref.shape[1]
    wide_ref[:, :width] = x_ref[...]
    terms, rest = [], weights
    for _ in range(3):
        terms.append(rest.astype(BF16))
        rest = rest - terms[-1].astype(F32)
    fill = wide_ref.shape[1] - width - 3 * count
    terms.append(jnp.zeros((w_ref.shape[0], fill), BF16))
    wide_ref[:, width:] = jnp.concatenate(terms, axis=1)
    pack_body(cap, ids_ref, x_ref, weights, outs, rows_ref)


def first(x, routes, gate_fixed, ids, cap, expert_count):
    rows, width = x.shape
    n = ids.shape[0]
    shape = jax.ShapeDtypeStruct((cap * FOLD, width // FOLD), x.dtype)
    return pl.pallas_call(
        functools.partial(first_kernel, n, cap),
        out_shape=(
            jax.ShapeDtypeStruct((rows, expert_count), F32),
            jax.ShapeDtypeStruct((rows, width + tail_width(expert_count)), BF16),
        )
        + (shape,) * n,
        in_specs=[SMEM, VMEM, VMEM, VMEM],
        out_specs=(VMEM,) * (2 + n),
        scratch_shapes=[pltpu.VMEM((n * heights(cap)[2], width), BF16)],
        compiler_params=pltpu.CompilerParams(vmem_limit_bytes=12 << 20),
        name="first",
    )(ids, x, routes, gate_fixed)


def pack_kernel(n, cap, ids_ref, wide_ref, *refs):
    w_ref, outs, rows_ref = refs[-2 - n], refs[-1 - n : -1], refs[-1]
    width, count = rows_ref.shape[1], w_ref.shape[1]
    shape = (wide_ref.shape[1] - width, count)
    r, c = iota(shape, 0), iota(shape, 1)
    add = ((r == c) | (r == c + count) | (r == c + 2 * count)).astype(BF16)
    weights = jnp.dot(wide_ref[:, width:], add, preferred_element_type=F32)
    w_ref[...] = weights
    pack_body(cap, ids_ref, wide_ref.at[:, :width], weights, outs, rows_ref)


def pack(wide, ids, cap, expert_count, after=()):
    rows = wide.shape[0]
    width = wide.shape[1] - tail_width(expert_count)
    n = ids.shape[0]
    shape = jax.ShapeDtypeStruct((cap * FOLD, width // FOLD), wide.dtype)
    return pl.pallas_call(
        functools.partial(pack_kernel, n, cap),
        out_shape=(jax.ShapeDtypeStruct((rows, expert_count), F32),) + (shape,) * n,
        in_specs=[SMEM, VMEM] + [ANY] * len(after),
        out_specs=(VMEM,) * (1 + n),
        scratch_shapes=[pltpu.VMEM((n * heights(cap)[2], width), BF16)],
        compiler_params=pltpu.CompilerParams(vmem_limit_bytes=12 << 20),
        name="pack",
    )(ids, wide, *after)


def expert_body(n, cap, blocks, weights, outs, x_ref, h_ref, y_ref, ready):
    high = heights(cap)[2]
    half, width = weights[2].shape[1:]
    for m in range(n):
        unfold(blocks[m], cap, x_ref, m * high)
    x = x_ref[...]
    steps = expert_steps(half, width)
    for i, (s, j) in enumerate(steps):
        ready(i)
        if s is not None:
            g, u = weights[3 * s : 3 * s + 2]
            gate = jnp.dot(x, g[0, :, j : j + TILE], preferred_element_type=F32)
            upper = jnp.dot(x, u[0, :, j : j + TILE], preferred_element_type=F32)
            hidden = gate / (1.0 + jnp.exp(-gate)) * upper
            h_ref[:, s * half + j : s * half + j + TILE] = hidden.astype(BF16)
        else:
            total = sum(
                jnp.dot(
                    h_ref[:, t * half : (t + 1) * half],
                    weights[3 * t + 2][0, :, j : j + 2 * TILE],
                    preferred_element_type=F32,
                )
                for t in range(2)
            )
            y_ref[:, j : j + 2 * TILE] = total.astype(BF16)
    for m in range(n):
        fold(y_ref, m * high, cap, outs[m])


def expert_steps(half, width):
    hidden = [(s, j) for s in range(2) for j in range(0, half, TILE)]
    return hidden + [(None, j) for j in range(0, width, 2 * TILE)]


def expert_kernel(n, cap, *refs):
    blocks, weights = refs[:n], refs[n : n + 6]
    outs, scratch = refs[-3 - n : -3], refs[-3:]
    expert_body(n, cap, blocks, weights, outs, *scratch, lambda i: None)


def expert_first_kernel(n, cap, *refs):
    blocks, sources = refs[:n], refs[n : n + 6]
    refs = refs[-4 - n - 6 :]
    outs, weights, scratch, sems = refs[:n], refs[n : n + 6], refs[n + 6 : -1], refs[-1]
    half, width = weights[2].shape[1:]
    steps = expert_steps(half, width)
    depth = sems.shape[0]

    def copies(i):
        s, j = steps[i]
        if s is not None:
            which, cols = (3 * s, 3 * s + 1), pl.ds(j, TILE)
        else:
            which, cols = (2, 5), pl.ds(j, 2 * TILE)
        return [
            pltpu.make_async_copy(
                sources[w].at[0, :, cols], weights[w].at[0, :, cols], sems.at[i % depth, t]
            )
            for t, w in enumerate(which)
        ]

    def ready(i):
        for copy in copies(i):
            copy.wait()
        if i + depth < len(steps):
            for copy in copies(i + depth):
                copy.start()

    for i in range(depth):
        for copy in copies(i):
            copy.start()
    expert_body(n, cap, blocks, weights, outs, *scratch, ready)


def expert(blocks, weights, cap, after=(), first_call=False):
    n = len(blocks)
    half, width = weights[2].shape[1:]
    rows = n * heights(cap)[2]
    out_shape = tuple(jax.ShapeDtypeStruct(b.shape, b.dtype) for b in blocks)
    scratch = [
        pltpu.VMEM((rows, width), BF16),
        pltpu.VMEM((rows, 2 * half), BF16),
        pltpu.VMEM((rows, width), BF16),
    ]
    if first_call:
        kernel, space, name = expert_first_kernel, ANY, "expert_first"
        out_shape += tuple(pltpu.VMEM(w.shape, w.dtype) for w in weights)
        scratch.append(pltpu.SemaphoreType.DMA((3, 2)))
    else:
        kernel, space, name = expert_kernel, VMEM, "expert"
        weights = [pltpu.with_memory_space_constraint(w, pltpu.VMEM) for w in weights]
    result = pl.pallas_call(
        functools.partial(kernel, n, cap),
        out_shape=out_shape,
        in_specs=[VMEM] * n + [space] * 6 + [ANY] * len(after),
        out_specs=(VMEM,) * len(out_shape),
        scratch_shapes=scratch,
        compiler_params=pltpu.CompilerParams(vmem_limit_bytes=18 << 20),
        name=name,
    )(*blocks, *weights, *after)
    return list(result[:n]), list(result[n:])


def combine_kernel(n, n_others, cap, ids_ref, w_ref, *refs):
    blocks, others = refs[:n], refs[n : n + n_others]
    out_ref, rows_ref = refs[-2:]
    tokens = out_ref.shape[0]
    high = heights(cap)[2]
    weights = w_ref[...]
    codes = slot_codes(weights)
    total = None
    for m in range(n):
        unfold(blocks[m], cap, rows_ref, m * high)
        code = column(codes, ids_ref[m]).astype(jnp.int32)
        pick = (code == iota((tokens, high), 1)).astype(BF16)
        rows = jnp.dot(pick, rows_ref[m * high : (m + 1) * high, :], preferred_element_type=F32)
        term = column(weights, ids_ref[m]) * rows
        total = term if total is None else total + term
    for other in others:
        total += other[...].astype(F32)
    out_ref[...] = total.astype(BF16)


def combine(blocks, weights, ids, cap, others=(), after=()):
    n = len(blocks)
    width = blocks[0].shape[1] * FOLD
    return pl.pallas_call(
        functools.partial(combine_kernel, n, len(others), cap),
        out_shape=jax.ShapeDtypeStruct((weights.shape[0], width), BF16),
        in_specs=[SMEM] + [VMEM] * (1 + n + len(others)) + [ANY] * len(after),
        out_specs=VMEM,
        scratch_shapes=[pltpu.VMEM((n * heights(cap)[2], width), BF16)],
        compiler_params=pltpu.CompilerParams(vmem_limit_bytes=12 << 20),
        name="combine",
    )(ids, weights, *blocks, *others, *after)


def on_device(tokens, routes, gate_fixed, w_gate, w_up, w_down):
    n_data = lax.axis_size("dp")
    n_owner = lax.axis_size("expert")
    line = n_owner // 2
    expert_count = n_data * line
    cap = 2 * (5 * tokens.shape[0] * TOP // (8 * expert_count) + 1)
    dp = lax.axis_index("dp")
    z = lax.axis_index("expert") // 2
    ids = jnp.stack([(dp ^ m) * line + z for m in range(n_data)]).astype(jnp.int32)

    def along(block, step):
        pairs = [(i, (i + 2 * step) % n_owner) for i in range(n_owner)]
        return lax.ppermute(block, "expert", pairs)

    def across(block, m):
        return lax.ppermute(block, "dp", [(i, i ^ m) for i in range(n_data)])

    def swap(block):
        return lax.ppermute(block, "expert", [(i, i ^ 1) for i in range(n_owner)])

    last = n_data - 1

    def exchange(lists, after=None):
        got = [lists[0]] + [across(lists[m], m) for m in range(1, last)]
        if last:
            got.append(across(tie(lists[last], *got[1:2]), last))
        return got

    weights, wide, *lists = first(tokens, routes, gate_fixed, ids, cap, expert_count)
    other = [swap(w_gate), swap(w_up)]
    ws, sent = [weights], [exchange(lists)]
    after = (*sent[0][1:last], *other)
    for k in range(1, line):
        wide = along(wide, 1)
        weights, *lists = pack(wide, ids, cap, expert_count, after=after)
        ws.append(weights)
        sent.append(exchange(lists))
        after = (*sent[k - 1][last:], *sent[k][1:last])
        if k == 1:
            other.append(swap(tie(w_down, lists[0])))
            after += (other[2],)
        if k == 2:
            held = [w_gate, w_up, w_down, *other]
            outs, held = expert(sent[0], held, cap, after=(lists[0],), first_call=True)
            result = {0: outs}
            after += (outs[0],)

    after = lists[:1]
    order = list(range(1, line))
    back = {}

    def send_back(k, after):
        part = combine(result[k], ws[k], ids, cap, after=after)
        back[k] = along(part, -k)
        return [part]

    for i, k in enumerate(order):
        if i >= 2:
            after = send_back(order[i - 2], after)
        outs, _ = expert(sent[k], held, cap, after=after)
        after = outs[:1]
        result[k] = [outs[0]] + [across(outs[m], m) for m in range(1, n_data)]
    result[0] = [result[0][0]] + [across(tie(result[0][m], after[0]), m) for m in range(1, n_data)]
    for k in order:
        if k not in back:
            send_back(k, after)
    return combine(result[0], ws[0], ids, cap, others=list(back.values()))


def solution(mesh):
    placed = (
        P(("dp", "expert"), None),
        P(("dp", "expert"), None),
        P(("dp", "expert"), None),
        P(("dp", "expert"), None, None),
        P(("dp", "expert"), None, None),
        P(("dp", "expert"), None, None),
    )
    return jax.shard_map(
        on_device, mesh=mesh, in_specs=placed, out_specs=P(("dp", "expert"), None), check_vma=False
    )
```

```python
import functools

import jax
import jax.numpy as jnp
from jax import lax
from jax.experimental import pallas as pl
from jax.experimental.pallas import tpu as pltpu
from jax.sharding import PartitionSpec as P

TOP = 8
FOLD = 8
SUB = 16
TILE = 256
SEQUENCE = ["P1", "P2", "E0", "P3", "E2", "E1", "C2", "E3", "C1", "C3"]
DEPS = {
    "S2": ["P1"],
    "P1": ["F0.1", "F0.2", "S0", "S1"],
    "F0.3": ["P1"],
    "F1.3": ["P2"],
    "P2": ["F0.3", "F1.1", "F1.2", "S2"],
    "P3": ["F1.3", "F2.1", "F2.2", "F2.3"],
    "R2.1": ["F3.1"],
    "R2.2": ["F3.2"],
    "R2.3": ["F3.3"],
    "R0.1": ["C1"],
    "R0.2": ["C1"],
    "R0.3": ["C1"],
}
VIA = {}
F32 = jnp.float32
BF16 = jnp.bfloat16
COST = pl.CostEstimate(flops=10**11, transcendentals=0, bytes_accessed=10**8)
VMEM = pl.BlockSpec(memory_space=pltpu.VMEM)
SMEM = pl.BlockSpec(memory_space=pltpu.SMEM)
ANY = pl.BlockSpec(memory_space=pl.ANY)


def iota(shape, dim):
    return lax.broadcasted_iota(jnp.int32, shape, dim)


def heights(cap):
    main = cap // SUB * SUB
    tail = cap - main
    return main, tail, main + (SUB if tail else 0)


def unfold(blocks, cap, rows_ref):
    main, tail, high = heights(cap)
    part = blocks[0].shape[1]
    if tail:
        shape = (FOLD * SUB, FOLD * tail)
        r, c = iota(shape, 0), iota(shape, 1)
        spread = ((r % SUB < tail) & (c == r // SUB * tail + r % SUB)).astype(BF16)
        ends = jnp.concatenate([block[FOLD * main :, :] for block in blocks], axis=1)
        last = jnp.dot(spread, ends, preferred_element_type=F32).astype(BF16)
    for m, block in enumerate(blocks):
        base = m * high
        for g in range(FOLD):
            cols = slice(g * part, (g + 1) * part)
            if main:
                rows_ref[base : base + main, cols] = block[g * main : (g + 1) * main, :]
            if tail:
                rows_ref[base + main : base + high, cols] = last[
                    g * SUB : (g + 1) * SUB, m * part : (m + 1) * part
                ]


def fold(rows_ref, cap, blocks):
    main, tail, high = heights(cap)
    part = blocks[0].shape[1]
    columns = [slice(g * part, (g + 1) * part) for g in range(FOLD)]
    if tail:
        starts = [m * high + main for m in range(len(blocks))]
        last = jnp.concatenate(
            [
                jnp.concatenate([rows_ref[at : at + SUB, cols] for cols in columns], axis=0)
                for at in starts
            ],
            axis=1,
        )
        shape = (FOLD * tail, FOLD * SUB)
        r, c = iota(shape, 0), iota(shape, 1)
        gather = ((c % SUB < tail) & (r == c // SUB * tail + c % SUB)).astype(BF16)
        ends = jnp.dot(gather, last, preferred_element_type=F32).astype(BF16)
    for m, block in enumerate(blocks):
        if main:
            for g, cols in enumerate(columns):
                block[g * main : (g + 1) * main, :] = rows_ref[m * high : m * high + main, cols]
        if tail:
            block[FOLD * main :, :] = ends[:, m * part : (m + 1) * part]


def slot_codes(weights):
    rows = weights.shape[0]
    named = weights > 0.0
    tri = (iota((rows, rows), 0) > iota((rows, rows), 1)).astype(BF16)
    slots = jnp.dot(tri, named.astype(BF16), preferred_element_type=F32)
    return jnp.where(named, slots, -1.0)


def column(values, which):
    return jnp.sum(jnp.where(iota(values.shape, 1) == which, values, 0.0), axis=1, keepdims=True)


def pack_body(cap, ids_ref, x_ref, weights, outs, rows_ref):
    tokens = x_ref.shape[0]
    high = heights(cap)[2]
    codes = slot_codes(weights)
    square = (tokens, tokens)
    picks = []
    for m in range(len(outs)):
        col = column(codes, ids_ref[m])
        row = jnp.sum(
            jnp.where(iota(square, 0) == iota(square, 1), col, 0.0), axis=0, keepdims=True
        ).astype(jnp.int32)
        picks.append((iota((high, tokens), 0) == row).astype(BF16))
    pick = jnp.concatenate(picks, axis=0)
    rows_ref[...] = jnp.dot(pick, x_ref[...], preferred_element_type=F32).astype(BF16)
    fold(rows_ref, cap, outs)


def tie(value, *others):
    return lax.optimization_barrier((value, *others))[0]


def tail_width(expert_count):
    return -(-3 * expert_count // 128) * 128


def first_kernel(n, cap, ids_ref, x_ref, routes_ref, gate_ref, *refs):
    w_ref, wide_ref, outs, rows_ref = refs[0], refs[1], refs[2 : 2 + n], refs[2 + n]
    tokens, width = x_ref.shape
    count = w_ref.shape[1]
    quant = gate_ref[...].astype(F32)
    chosen = quant / jnp.sum(quant, axis=0, keepdims=True)
    routes = routes_ref[...]
    experts = iota((count, tokens), 0)
    turned = jnp.zeros((count, tokens), F32)
    for k in range(TOP):
        turned += jnp.where(experts == routes[k : k + 1, :], chosen[k : k + 1, :], 0.0)
    unit = (iota((tokens, tokens), 0) == iota((tokens, tokens), 1)).astype(BF16)
    terms, rest = [], turned
    for _ in range(3):
        term = rest.astype(BF16)
        rest = rest - term.astype(F32)
        terms.append(lax.dot_general(unit, term, (((1,), (1,)), ((), ())), preferred_element_type=F32))
    weights = terms[0] + terms[1] + terms[2]
    w_ref[...] = weights
    wide_ref[:, :width] = x_ref[...]
    terms.append(jnp.zeros((tokens, wide_ref.shape[1] - width - 3 * count), F32))
    wide_ref[:, width:] = jnp.concatenate(terms, axis=1).astype(BF16)
    pack_body(cap, ids_ref, x_ref, weights, outs, rows_ref)


def first(x, routes, gate_fixed, ids, cap, expert_count):
    rows, width = x.shape
    n = ids.shape[0]
    shape = jax.ShapeDtypeStruct((cap * FOLD, width // FOLD), x.dtype)
    return pl.pallas_call(
        functools.partial(first_kernel, n, cap),
        out_shape=(
            jax.ShapeDtypeStruct((rows, expert_count), F32),
            jax.ShapeDtypeStruct((rows, width + tail_width(expert_count)), BF16),
        )
        + (shape,) * n,
        in_specs=[SMEM, VMEM, VMEM, VMEM],
        out_specs=(VMEM,) * (2 + n),
        scratch_shapes=[pltpu.VMEM((n * heights(cap)[2], width), BF16)],
        cost_estimate=COST,
        compiler_params=pltpu.CompilerParams(vmem_limit_bytes=12 << 20),
        name="first",
    )(ids, x, routes.T, gate_fixed.T)


def pack_kernel(n, cap, ids_ref, wide_ref, *refs):
    w_ref, outs, rows_ref = refs[-2 - n], refs[-1 - n : -1], refs[-1]
    width, count = rows_ref.shape[1], w_ref.shape[1]
    shape = (wide_ref.shape[1] - width, count)
    r, c = iota(shape, 0), iota(shape, 1)
    add = ((r == c) | (r == c + count) | (r == c + 2 * count)).astype(BF16)
    weights = jnp.dot(wide_ref[:, width:], add, preferred_element_type=F32)
    w_ref[...] = weights
    pack_body(cap, ids_ref, wide_ref.at[:, :width], weights, outs, rows_ref)


def pack(wide, ids, cap, expert_count, after=()):
    rows = wide.shape[0]
    width = wide.shape[1] - tail_width(expert_count)
    n = ids.shape[0]
    shape = jax.ShapeDtypeStruct((cap * FOLD, width // FOLD), wide.dtype)
    return pl.pallas_call(
        functools.partial(pack_kernel, n, cap),
        out_shape=(jax.ShapeDtypeStruct((rows, expert_count), F32),) + (shape,) * n,
        in_specs=[SMEM, VMEM] + [ANY] * len(after),
        out_specs=(VMEM,) * (1 + n),
        scratch_shapes=[pltpu.VMEM((n * heights(cap)[2], width), BF16)],
        cost_estimate=COST,
        compiler_params=pltpu.CompilerParams(vmem_limit_bytes=12 << 20),
        name="pack",
    )(ids, wide, *after)


def expert_body(cap, blocks, weights, outs, x_ref, h_ref, y_ref, ready):
    half, width = weights[2].shape[1:]
    unfold(blocks, cap, x_ref)
    x = x_ref[...]
    steps = expert_steps(half, width)
    for i, (s, j) in enumerate(steps):
        ready(i)
        if s is not None:
            g, u = weights[3 * s : 3 * s + 2]
            gate = jnp.dot(x, g[0, :, j : j + TILE], preferred_element_type=F32)
            upper = jnp.dot(x, u[0, :, j : j + TILE], preferred_element_type=F32)
            hidden = gate / (1.0 + jnp.exp(-gate)) * upper
            h_ref[:, s * half + j : s * half + j + TILE] = hidden.astype(BF16)
        else:
            total = sum(
                jnp.dot(
                    h_ref[:, t * half : (t + 1) * half],
                    weights[3 * t + 2][0, :, j : j + 2 * TILE],
                    preferred_element_type=F32,
                )
                for t in range(2)
            )
            y_ref[:, j : j + 2 * TILE] = total.astype(BF16)
    fold(y_ref, cap, outs)


def expert_steps(half, width):
    hidden = [(s, j) for s in range(2) for j in range(0, half, TILE)]
    return hidden + [(None, j) for j in range(0, width, 2 * TILE)]


def expert_kernel(n, cap, *refs):
    blocks, weights = refs[:n], refs[n : n + 6]
    outs, scratch = refs[-3 - n : -3], refs[-3:]
    expert_body(cap, blocks, weights, outs, *scratch, lambda i: None)


def expert_first_kernel(n, cap, *refs):
    blocks, sources = refs[:n], refs[n : n + 6]
    refs = refs[-4 - n - 6 :]
    outs, weights, scratch, sems = refs[:n], refs[n : n + 6], refs[n + 6 : -1], refs[-1]
    half, width = weights[2].shape[1:]
    steps = expert_steps(half, width)
    depth = sems.shape[0]

    def copies(i):
        s, j = steps[i]
        if s is not None:
            which, cols = (3 * s, 3 * s + 1), pl.ds(j, TILE)
        else:
            which, cols = (2, 5), pl.ds(j, 2 * TILE)
        return [
            pltpu.make_async_copy(
                sources[w].at[0, :, cols], weights[w].at[0, :, cols], sems.at[i % depth, t]
            )
            for t, w in enumerate(which)
        ]

    def ready(i):
        for copy in copies(i):
            copy.wait()
        if i + depth < len(steps):
            for copy in copies(i + depth):
                copy.start()

    for i in range(depth):
        for copy in copies(i):
            copy.start()
    expert_body(cap, blocks, weights, outs, *scratch, ready)


def expert(blocks, weights, cap, after=(), first_call=False):
    n = len(blocks)
    half, width = weights[2].shape[1:]
    rows = n * heights(cap)[2]
    out_shape = tuple(jax.ShapeDtypeStruct(b.shape, b.dtype) for b in blocks)
    scratch = [
        pltpu.VMEM((rows, width), BF16),
        pltpu.VMEM((rows, 2 * half), BF16),
        pltpu.VMEM((rows, width), BF16),
    ]
    if first_call:
        kernel, space, name = expert_first_kernel, ANY, "expert_first"
        out_shape += tuple(pltpu.VMEM(w.shape, w.dtype) for w in weights)
        scratch.append(pltpu.SemaphoreType.DMA((5, 2)))
    else:
        kernel, space, name = expert_kernel, VMEM, "expert"
        weights = [pltpu.with_memory_space_constraint(w, pltpu.VMEM) for w in weights]
    result = pl.pallas_call(
        functools.partial(kernel, n, cap),
        out_shape=out_shape,
        in_specs=[VMEM] * n + [space] * 6 + [ANY] * len(after),
        out_specs=(VMEM,) * len(out_shape),
        scratch_shapes=scratch,
        cost_estimate=COST,
        compiler_params=pltpu.CompilerParams(vmem_limit_bytes=18 << 20),
        name=name,
    )(*blocks, *weights, *after)
    return list(result[:n]), list(result[n:])


def combine_kernel(n, n_others, cap, ids_ref, w_ref, *refs):
    blocks, others = refs[:n], refs[n : n + n_others]
    out_ref, rows_ref = refs[-2:]
    tokens = out_ref.shape[0]
    high = heights(cap)[2]
    weights = w_ref[...]
    codes = slot_codes(weights)
    total = None
    unfold(blocks, cap, rows_ref)
    for m in range(n):
        code = column(codes, ids_ref[m]).astype(jnp.int32)
        pick = (code == iota((tokens, high), 1)).astype(BF16)
        rows = jnp.dot(pick, rows_ref[m * high : (m + 1) * high, :], preferred_element_type=F32)
        term = column(weights, ids_ref[m]) * rows
        total = term if total is None else total + term
    for other in others:
        total += other[...].astype(F32)
    out_ref[...] = total.astype(BF16)


def combine(blocks, weights, ids, cap, others=(), after=()):
    n = len(blocks)
    width = blocks[0].shape[1] * FOLD
    return pl.pallas_call(
        functools.partial(combine_kernel, n, len(others), cap),
        out_shape=jax.ShapeDtypeStruct((weights.shape[0], width), BF16),
        in_specs=[SMEM] + [VMEM] * (1 + n + len(others)) + [ANY] * len(after),
        out_specs=VMEM,
        scratch_shapes=[pltpu.VMEM((n * heights(cap)[2], width), BF16)],
        cost_estimate=COST,
        compiler_params=pltpu.CompilerParams(vmem_limit_bytes=12 << 20),
        name="combine",
    )(ids, weights, *blocks, *others, *after)


def plan(line, n_data):
    if line == 4 and n_data == 4:
        return SEQUENCE, DEPS, VIA
    far = sorted(range(1, line), key=lambda k: (-min(k, line - k), k))
    steps = [f"P{k}" for k in range(1, line)] + [f"E{k}" for k in far + [0]]
    return steps + [f"C{k}" for k in far], {}, {}


def on_device(tokens, routes, gate_fixed, w_gate, w_up, w_down):
    n_data = lax.axis_size("dp")
    n_owner = lax.axis_size("expert")
    line = n_owner // 2
    expert_count = n_data * line
    cap = 2 * (5 * tokens.shape[0] * TOP // (8 * expert_count) + 1)
    dp = lax.axis_index("dp")
    z = lax.axis_index("expert") // 2
    ids = jnp.stack([(dp ^ m) * line + z for m in range(n_data)]).astype(jnp.int32)
    sequence, deps, via = plan(line, n_data)
    made = {}

    def along(block, step):
        pairs = [(i, (i + 2 * step) % n_owner) for i in range(n_owner)]
        return lax.ppermute(block, "expert", pairs)

    def across(block, m):
        return lax.ppermute(block, "dp", [(i, i ^ m) for i in range(n_data)])

    def swap(block):
        return lax.ppermute(block, "expert", [(i, i ^ 1) for i in range(n_owner)])

    def marks(name):
        step = get(name)
        return step if isinstance(step, jax.Array) else step[-1]

    def after(name):
        at = sequence.index(name) if name in sequence else 0
        return [marks(d) for d in [*sequence[:at][-1:], *deps.get(name, ())]]

    def held(value, name):
        others = [marks(d) for d in deps.get(name, ())]
        return tie(value, *others) if others else value

    def lists(kind, k):
        source = get(("P" if kind == "F" else "E") + str(k))
        return [source[0]] + [get(f"{kind}{k}.{m}") for m in range(1, n_data)]

    def get(name):
        if name not in made:
            made[name] = make(name, name[0], *map(int, name[1:].split(".")))
        return made[name]

    def make(name, kind, k, m=0):
        if kind == "S":
            return swap(held((w_gate, w_up, w_down)[k], name))
        if kind == "X":
            return along(held(get("P0")[-2] if k == 1 else get(f"X{k - 1}"), name), 1)
        if kind == "P" and k == 0:
            weights, wide, *outs = first(tokens, routes, gate_fixed, ids, cap, expert_count)
            return [*outs, weights, wide, outs[0]]
        if kind == "P":
            weights, *outs = pack(get(f"X{k}"), ids, cap, expert_count, after=after(name))
            return [*outs, weights, outs[0]]
        if kind in "FR":
            return across(held(get(("P" if kind == "F" else "E") + str(k))[m], name), m)
        if kind == "E":
            opening = next(s for s in sequence if s[0] == "E")
            if name == opening:
                weights = [w_gate, w_up, w_down] + [get(f"S{i}") for i in range(3)]
            else:
                weights = get(opening)[n_data:-1]
            outs, kept = expert(lists("F", k), weights, cap, after=after(name), first_call=name == opening)
            return [*outs, *kept, outs[0]]
        if kind == "C":
            others = [get(f"H{far}") for far, near in via.items() if near == k]
            return combine(lists("R", k), get(f"P{k}")[n_data], ids, cap, others=others, after=after(name))
        return along(held(get(f"C{k}"), name), via.get(k, 0) - k)

    for name in sequence:
        get(name)
    ends = [get(f"H{k}") for k in range(1, line) if k not in via]
    return combine(lists("R", 0), get("P0")[n_data], ids, cap, others=ends)


def solution(mesh):
    placed = (
        P(("dp", "expert"), None),
        P(("dp", "expert"), None),
        P(("dp", "expert"), None),
        P(("dp", "expert"), None, None),
        P(("dp", "expert"), None, None),
        P(("dp", "expert"), None, None),
    )
    return jax.shard_map(
        on_device, mesh=mesh, in_specs=placed, out_specs=P(("dp", "expert"), None), check_vma=False
    )
```

```python
import functools

import jax
import jax.numpy as jnp
from jax import lax
from jax.experimental import pallas as pl
from jax.experimental.pallas import tpu as pltpu
from jax.sharding import PartitionSpec as P

TOP = 8
FOLD = 8
SUB = 16
TILE = 256
SEQUENCE = ["P1", "P2", "E0", "P3", "E2", "E1", "C2", "E3", "C1", "C3"]
DEPS = {
    "S2": ["P1"],
    "P1": ["F0.1", "F0.2", "S0", "S1"],
    "F0.3": ["P1"],
    "F1.3": ["P2"],
    "P2": ["F0.3", "F1.1", "F1.2", "S2"],
    "P3": ["F1.3", "F2.1"],
    "R2.1": ["F3.1"],
    "R2.2": ["F3.2"],
    "R2.3": ["F3.3"],
    "R0.1": ["C1"],
    "R0.2": ["C1"],
    "R0.3": ["C1"],
}
VIA = {}
F32 = jnp.float32
BF16 = jnp.bfloat16
COST = pl.CostEstimate(flops=12 * 10**9, transcendentals=0, bytes_accessed=10**8)
VMEM = pl.BlockSpec(memory_space=pltpu.VMEM)
SMEM = pl.BlockSpec(memory_space=pltpu.SMEM)
ANY = pl.BlockSpec(memory_space=pl.ANY)


def iota(shape, dim):
    return lax.broadcasted_iota(jnp.int32, shape, dim)


def heights(cap):
    main = cap // SUB * SUB
    tail = cap - main
    return main, tail, main + (SUB if tail else 0)


def unfold(blocks, cap, rows_ref):
    main, tail, high = heights(cap)
    part = blocks[0].shape[1]
    if tail:
        shape = (FOLD * SUB, FOLD * tail)
        r, c = iota(shape, 0), iota(shape, 1)
        spread = ((r % SUB < tail) & (c == r // SUB * tail + r % SUB)).astype(BF16)
        ends = jnp.concatenate([block[FOLD * main :, :] for block in blocks], axis=1)
        last = jnp.dot(spread, ends, preferred_element_type=F32).astype(BF16)
    for m, block in enumerate(blocks):
        base = m * high
        for g in range(FOLD):
            cols = slice(g * part, (g + 1) * part)
            if main:
                rows_ref[base : base + main, cols] = block[g * main : (g + 1) * main, :]
            if tail:
                rows_ref[base + main : base + high, cols] = last[
                    g * SUB : (g + 1) * SUB, m * part : (m + 1) * part
                ]


def fold(rows_ref, cap, blocks):
    main, tail, high = heights(cap)
    part = blocks[0].shape[1]
    columns = [slice(g * part, (g + 1) * part) for g in range(FOLD)]
    if tail:
        starts = [m * high + main for m in range(len(blocks))]
        last = jnp.concatenate(
            [
                jnp.concatenate([rows_ref[at : at + SUB, cols] for cols in columns], axis=0)
                for at in starts
            ],
            axis=1,
        )
        shape = (FOLD * tail, FOLD * SUB)
        r, c = iota(shape, 0), iota(shape, 1)
        gather = ((c % SUB < tail) & (r == c // SUB * tail + c % SUB)).astype(BF16)
        ends = jnp.dot(gather, last, preferred_element_type=F32).astype(BF16)
    for m, block in enumerate(blocks):
        if main:
            for g, cols in enumerate(columns):
                block[g * main : (g + 1) * main, :] = rows_ref[m * high : m * high + main, cols]
        if tail:
            block[FOLD * main :, :] = ends[:, m * part : (m + 1) * part]


def tight(cap, n):
    main, tail, _ = heights(cap)
    ends = -(-n * tail // SUB) * SUB
    return n * main + ends, ends


def quotient(value, divisor):
    return ((value.astype(F32) + 0.5) * (1.0 / divisor)).astype(jnp.int32)


def unfold_tight(blocks, cap, rows_ref):
    main, tail, _ = heights(cap)
    n, part = len(blocks), blocks[0].shape[1]
    high, ends = tight(cap, n)
    if tail:
        r = iota((FOLD * ends, 1), 0)
        g = quotient(r, ends)
        q = r - g * ends
        m = quotient(q, tail)
        source = jnp.where(q < n * tail, m * (FOLD * tail) + g * tail + q - m * tail, -1)
        spread = (iota((FOLD * ends, n * FOLD * tail), 1) == source).astype(BF16)
        tails = jnp.concatenate([block[FOLD * main :, :] for block in blocks], axis=0)
        last = jnp.dot(spread, tails, preferred_element_type=F32).astype(BF16)
    for g in range(FOLD):
        cols = slice(g * part, (g + 1) * part)
        if main:
            for m, block in enumerate(blocks):
                rows_ref[m * main : (m + 1) * main, cols] = block[g * main : (g + 1) * main, :]
        if tail:
            rows_ref[high - ends : high, cols] = last[g * ends : (g + 1) * ends]


def fold_tight(rows_ref, cap, blocks):
    main, tail, _ = heights(cap)
    n, part = len(blocks), blocks[0].shape[1]
    high, ends = tight(cap, n)
    columns = [slice(g * part, (g + 1) * part) for g in range(FOLD)]
    if tail:
        r = iota((n * FOLD * tail, 1), 0)
        m = quotient(r, FOLD * tail)
        rest = r - m * (FOLD * tail)
        g = quotient(rest, tail)
        source = g * ends + m * tail + rest - g * tail
        gather = (iota((n * FOLD * tail, FOLD * ends), 1) == source).astype(BF16)
        last = jnp.concatenate([rows_ref[high - ends : high, cols] for cols in columns], axis=0)
        tails = jnp.dot(gather, last, preferred_element_type=F32).astype(BF16)
    for m, block in enumerate(blocks):
        if main:
            for g, cols in enumerate(columns):
                block[g * main : (g + 1) * main, :] = rows_ref[m * main : (m + 1) * main, cols]
        if tail:
            block[FOLD * main :, :] = tails[m * FOLD * tail : (m + 1) * FOLD * tail]


def slot_codes(weights):
    rows = weights.shape[0]
    named = weights > 0.0
    tri = (iota((rows, rows), 0) > iota((rows, rows), 1)).astype(BF16)
    slots = jnp.dot(tri, named.astype(BF16), preferred_element_type=F32)
    return jnp.where(named, slots, -1.0)


def column(values, which):
    return jnp.sum(jnp.where(iota(values.shape, 1) == which, values, 0.0), axis=1, keepdims=True)


def pack_body(cap, ids_ref, x_ref, weights, outs, rows_ref):
    tokens = x_ref.shape[0]
    high = heights(cap)[2]
    codes = slot_codes(weights)
    square = (tokens, tokens)
    picks = []
    for m in range(len(outs)):
        col = column(codes, ids_ref[m])
        row = jnp.sum(
            jnp.where(iota(square, 0) == iota(square, 1), col, 0.0), axis=0, keepdims=True
        ).astype(jnp.int32)
        picks.append((iota((high, tokens), 0) == row).astype(BF16))
    pick = jnp.concatenate(picks, axis=0)
    rows_ref[...] = jnp.dot(pick, x_ref[...], preferred_element_type=F32).astype(BF16)
    fold(rows_ref, cap, outs)


def tie(value, *others):
    return lax.optimization_barrier((value, *others))[0]


def tail_width(expert_count):
    return -(-3 * expert_count // 128) * 128


def first_kernel(n, cap, ids_ref, x_ref, routes_ref, gate_ref, *refs):
    w_ref, wide_ref, outs, rows_ref = refs[0], refs[1], refs[2 : 2 + n], refs[2 + n]
    tokens, width = x_ref.shape
    count = w_ref.shape[1]
    quant = gate_ref[...].astype(F32)
    chosen = quant / jnp.sum(quant, axis=0, keepdims=True)
    routes = routes_ref[...]
    experts = iota((count, tokens), 0)
    turned = jnp.zeros((count, tokens), F32)
    for k in range(TOP):
        turned += jnp.where(experts == routes[k : k + 1, :], chosen[k : k + 1, :], 0.0)
    unit = (iota((tokens, tokens), 0) == iota((tokens, tokens), 1)).astype(BF16)
    terms, rest = [], turned
    for _ in range(3):
        term = rest.astype(BF16)
        rest = rest - term.astype(F32)
        terms.append(lax.dot_general(unit, term, (((1,), (1,)), ((), ())), preferred_element_type=F32))
    weights = terms[0] + terms[1] + terms[2]
    w_ref[...] = weights
    wide_ref[:, :width] = x_ref[...]
    terms.append(jnp.zeros((tokens, wide_ref.shape[1] - width - 3 * count), F32))
    wide_ref[:, width:] = jnp.concatenate(terms, axis=1).astype(BF16)
    pack_body(cap, ids_ref, x_ref, weights, outs, rows_ref)


def first(x, routes, gate_fixed, ids, cap, expert_count):
    rows, width = x.shape
    n = ids.shape[0]
    shape = jax.ShapeDtypeStruct((cap * FOLD, width // FOLD), x.dtype)
    return pl.pallas_call(
        functools.partial(first_kernel, n, cap),
        out_shape=(
            jax.ShapeDtypeStruct((rows, expert_count), F32),
            jax.ShapeDtypeStruct((rows, width + tail_width(expert_count)), BF16),
        )
        + (shape,) * n,
        in_specs=[SMEM, VMEM, VMEM, VMEM],
        out_specs=(VMEM,) * (2 + n),
        scratch_shapes=[pltpu.VMEM((n * heights(cap)[2], width), BF16)],
        cost_estimate=COST,
        compiler_params=pltpu.CompilerParams(vmem_limit_bytes=12 << 20),
        name="first",
    )(ids, *[pltpu.with_memory_space_constraint(a, pltpu.HBM) for a in (x, routes.T, gate_fixed.T)])


def pack_kernel(n, cap, ids_ref, wide_ref, *refs):
    w_ref, outs, rows_ref = refs[-2 - n], refs[-1 - n : -1], refs[-1]
    width, count = rows_ref.shape[1], w_ref.shape[1]
    shape = (wide_ref.shape[1] - width, count)
    r, c = iota(shape, 0), iota(shape, 1)
    add = ((r == c) | (r == c + count) | (r == c + 2 * count)).astype(BF16)
    weights = jnp.dot(wide_ref[:, width:], add, preferred_element_type=F32)
    w_ref[...] = weights
    pack_body(cap, ids_ref, wide_ref.at[:, :width], weights, outs, rows_ref)


def pack(wide, ids, cap, expert_count, after=()):
    rows = wide.shape[0]
    width = wide.shape[1] - tail_width(expert_count)
    n = ids.shape[0]
    shape = jax.ShapeDtypeStruct((cap * FOLD, width // FOLD), wide.dtype)
    return pl.pallas_call(
        functools.partial(pack_kernel, n, cap),
        out_shape=(jax.ShapeDtypeStruct((rows, expert_count), F32),) + (shape,) * n,
        in_specs=[SMEM, VMEM] + [ANY] * len(after),
        out_specs=(VMEM,) * (1 + n),
        scratch_shapes=[pltpu.VMEM((n * heights(cap)[2], width), BF16)],
        cost_estimate=COST,
        compiler_params=pltpu.CompilerParams(vmem_limit_bytes=12 << 20),
        name="pack",
    )(ids, wide, *after)


def expert_body(cap, blocks, weights, outs, x_ref, h_ref, y_ref, ready):
    half, width = weights[2].shape[1:]
    unfold_tight(blocks, cap, x_ref)
    x = x_ref[...]
    steps = expert_steps(half, width)
    for i, (s, j) in enumerate(steps):
        ready(i)
        if s is not None:
            g, u = weights[3 * s : 3 * s + 2]
            gate = jnp.dot(x, g[0, :, j : j + TILE], preferred_element_type=F32)
            upper = jnp.dot(x, u[0, :, j : j + TILE], preferred_element_type=F32)
            hidden = gate / (1.0 + jnp.exp(-gate)) * upper
            h_ref[:, s * half + j : s * half + j + TILE] = hidden.astype(BF16)
        else:
            total = sum(
                jnp.dot(
                    h_ref[:, t * half : (t + 1) * half],
                    weights[3 * t + 2][0, :, j : j + 2 * TILE],
                    preferred_element_type=F32,
                )
                for t in range(2)
            )
            y_ref[:, j : j + 2 * TILE] = total.astype(BF16)
    fold_tight(y_ref, cap, outs)


def expert_steps(half, width):
    hidden = [(s, j) for s in range(2) for j in range(0, half, TILE)]
    return hidden + [(None, j) for j in range(0, width, 2 * TILE)]


def expert_kernel(n, cap, *refs):
    blocks, weights = refs[:n], refs[n : n + 6]
    outs, scratch = refs[-3 - n : -3], refs[-3:]
    expert_body(cap, blocks, weights, outs, *scratch, lambda i: None)


def expert_first_kernel(n, cap, *refs):
    blocks, sources = refs[:n], refs[n : n + 6]
    refs = refs[-4 - n - 6 :]
    outs, weights, scratch, sems = refs[:n], refs[n : n + 6], refs[n + 6 : -1], refs[-1]
    half, width = weights[2].shape[1:]
    steps = expert_steps(half, width)
    depth = sems.shape[0]

    def copies(i):
        s, j = steps[i]
        if s is not None:
            which, cols = (3 * s, 3 * s + 1), pl.ds(j, TILE)
        else:
            which, cols = (2, 5), pl.ds(j, 2 * TILE)
        return [
            pltpu.make_async_copy(
                sources[w].at[0, :, cols], weights[w].at[0, :, cols], sems.at[i % depth, t]
            )
            for t, w in enumerate(which)
        ]

    def ready(i):
        for copy in copies(i):
            copy.wait()
        if i + depth < len(steps):
            for copy in copies(i + depth):
                copy.start()

    for i in range(depth):
        for copy in copies(i):
            copy.start()
    expert_body(cap, blocks, weights, outs, *scratch, ready)


def expert(blocks, weights, cap, after=(), first_call=False):
    n = len(blocks)
    half, width = weights[2].shape[1:]
    rows = tight(cap, n)[0]
    out_shape = tuple(jax.ShapeDtypeStruct(b.shape, b.dtype) for b in blocks)
    scratch = [
        pltpu.VMEM((rows, width), BF16),
        pltpu.VMEM((rows, 2 * half), BF16),
        pltpu.VMEM((rows, width), BF16),
    ]
    if first_call:
        kernel, space, name = expert_first_kernel, ANY, "expert_first"
        out_shape += tuple(pltpu.VMEM(w.shape, w.dtype) for w in weights)
        scratch.append(pltpu.SemaphoreType.DMA((5, 2)))
    else:
        kernel, space, name = expert_kernel, VMEM, "expert"
        weights = [pltpu.with_memory_space_constraint(w, pltpu.VMEM) for w in weights]
    result = pl.pallas_call(
        functools.partial(kernel, n, cap),
        out_shape=out_shape,
        in_specs=[VMEM] * n + [space] * 6 + [ANY] * len(after),
        out_specs=(VMEM,) * len(out_shape),
        scratch_shapes=scratch,
        cost_estimate=COST,
        compiler_params=pltpu.CompilerParams(vmem_limit_bytes=18 << 20),
        name=name,
    )(*blocks, *weights, *after)
    return list(result[:n]), list(result[n:])


def combine_kernel(n, n_others, cap, ids_ref, w_ref, *refs):
    blocks, others = refs[:n], refs[n : n + n_others]
    out_ref, rows_ref = refs[-2:]
    tokens = out_ref.shape[0]
    high = heights(cap)[2]
    weights = w_ref[...]
    codes = slot_codes(weights)
    total = None
    unfold(blocks, cap, rows_ref)
    for m in range(n):
        code = column(codes, ids_ref[m]).astype(jnp.int32)
        pick = (code == iota((tokens, high), 1)).astype(BF16)
        rows = jnp.dot(pick, rows_ref[m * high : (m + 1) * high, :], preferred_element_type=F32)
        term = column(weights, ids_ref[m]) * rows
        total = term if total is None else total + term
    for other in others:
        total += other[...].astype(F32)
    out_ref[...] = total.astype(BF16)


def combine(blocks, weights, ids, cap, others=(), after=()):
    n = len(blocks)
    width = blocks[0].shape[1] * FOLD
    return pl.pallas_call(
        functools.partial(combine_kernel, n, len(others), cap),
        out_shape=jax.ShapeDtypeStruct((weights.shape[0], width), BF16),
        in_specs=[SMEM] + [VMEM] * (1 + n + len(others)) + [ANY] * len(after),
        out_specs=VMEM,
        scratch_shapes=[pltpu.VMEM((n * heights(cap)[2], width), BF16)],
        cost_estimate=COST,
        compiler_params=pltpu.CompilerParams(vmem_limit_bytes=12 << 20),
        name="combine",
    )(ids, weights, *blocks, *others, *after)


def plan(line, n_data):
    if line == 4 and n_data == 4:
        return SEQUENCE, DEPS, VIA
    far = sorted(range(1, line), key=lambda k: (-min(k, line - k), k))
    steps = [f"P{k}" for k in range(1, line)] + [f"E{k}" for k in far + [0]]
    return steps + [f"C{k}" for k in far], {}, {}


def on_device(tokens, routes, gate_fixed, w_gate, w_up, w_down):
    n_data = lax.axis_size("dp")
    n_owner = lax.axis_size("expert")
    line = n_owner // 2
    expert_count = n_data * line
    cap = 2 * (5 * tokens.shape[0] * TOP // (8 * expert_count) + 1)
    dp = lax.axis_index("dp")
    z = lax.axis_index("expert") // 2
    ids = jnp.stack([(dp ^ m) * line + z for m in range(n_data)]).astype(jnp.int32)
    sequence, deps, via = plan(line, n_data)
    made = {}

    def along(block, step):
        pairs = [(i, (i + 2 * step) % n_owner) for i in range(n_owner)]
        return lax.ppermute(block, "expert", pairs)

    def across(block, m):
        return lax.ppermute(block, "dp", [(i, i ^ m) for i in range(n_data)])

    def swap(block):
        return lax.ppermute(block, "expert", [(i, i ^ 1) for i in range(n_owner)])

    def marks(name):
        step = get(name)
        return step if isinstance(step, jax.Array) else step[-1]

    def after(name):
        at = sequence.index(name) if name in sequence else 0
        return [marks(d) for d in [*sequence[:at][-1:], *deps.get(name, ())]]

    def held(value, name):
        others = [marks(d) for d in deps.get(name, ())]
        return tie(value, *others) if others else value

    def lists(kind, k):
        source = get(("P" if kind == "F" else "E") + str(k))
        return [source[0]] + [get(f"{kind}{k}.{m}") for m in range(1, n_data)]

    def get(name):
        if name not in made:
            made[name] = make(name, name[0], *map(int, name[1:].split(".")))
        return made[name]

    def make(name, kind, k, m=0):
        if kind == "S":
            return swap(held((w_gate, w_up, w_down)[k], name))
        if kind == "X":
            return along(held(get("P0")[-2] if k == 1 else get(f"X{k - 1}"), name), 1)
        if kind == "P" and k == 0:
            weights, wide, *outs = first(tokens, routes, gate_fixed, ids, cap, expert_count)
            return [*outs, weights, wide, outs[0]]
        if kind == "P":
            weights, *outs = pack(get(f"X{k}"), ids, cap, expert_count, after=after(name))
            return [*outs, weights, outs[0]]
        if kind in "FR":
            return across(held(get(("P" if kind == "F" else "E") + str(k))[m], name), m)
        if kind == "E":
            opening = next(s for s in sequence if s[0] == "E")
            if name == opening:
                weights = [w_gate, w_up, w_down] + [get(f"S{i}") for i in range(3)]
            else:
                weights = get(opening)[n_data:-1]
            outs, kept = expert(lists("F", k), weights, cap, after=after(name), first_call=name == opening)
            return [*outs, *kept, outs[0]]
        if kind == "C":
            others = [get(f"H{far}") for far, near in via.items() if near == k]
            return combine(lists("R", k), get(f"P{k}")[n_data], ids, cap, others=others, after=after(name))
        return along(held(get(f"C{k}"), name), via.get(k, 0) - k)

    for name in sequence:
        get(name)
    ends = [get(f"H{k}") for k in range(1, line) if k not in via]
    return combine(lists("R", 0), get("P0")[n_data], ids, cap, others=ends)


def solution(mesh):
    placed = (
        P(("dp", "expert"), None),
        P(("dp", "expert"), None),
        P(("dp", "expert"), None),
        P(("dp", "expert"), None, None),
        P(("dp", "expert"), None, None),
        P(("dp", "expert"), None, None),
    )
    return jax.shard_map(
        on_device, mesh=mesh, in_specs=placed, out_specs=P(("dp", "expert"), None), check_vma=False
    )
```
